32 devices in a mesh: fft: 8 (over z, x), chan: 4 (over y, core).
Axes of the slice: x: 2, y: 2, z: 4, core: 2. Of those that a mesh axis runs over, the one named last changes fastest.
Arguments:
- visibilities: float32 [32, 2, 32, 128], P(('fft', 'chan')), may hold values from -6 to 6
- positions: float32 [32, 2, 32, 128], P(('fft', 'chan')), may hold values from 0 to 1
- cell_row: int32 [32, 32, 128], P(('fft', 'chan')), may hold values from 4 to 59
- cell_column: int32 [32, 32, 128], P(('fft', 'chan')), may hold values from 4 to 1019
- kernel_class: int32 [32, 32, 128], P(('fft', 'chan')), may hold values from 0 to 3
- send_counts: int32 [32, 32], P(('fft', 'chan')), may hold values from 96 to 128, as said below
- tile_lists: int32 [32, 8, 384], P(('fft', 'chan')), may hold values from 0 to 4095, as said below
- tile_counts: int32 [32, 8], P(('fft', 'chan')), may hold values from 192 to 384, as said below
- model_image: float32 [8, 128, 32768], P('chan', 'fft'), may hold values from -6 to 6
- threshold: float32 [8], P('chan'), may hold values from 0.5 to 3
Outputs:
- updated_model: float32 [8, 128, 32768], P('chan', 'fft')
- residuals: float32 [32, 2, 32, 128], P(('fft', 'chan'))
The draws below stay inside these ranges and needn't reach their ends.
Inputs may be any that keep to these rules, and one draw needn't show every extreme that they name: `send_counts`: for each receiver some sender uses all 128 slots to it. `tile_lists`: entries below a list's count name slots p of sender s with p < send_counts[s, d] for the receiver d, and no slot is named twice among the entries below the counts of one receiver; other entries are arbitrary slot numbers. `tile_counts`: on every receiver one list has exactly 384 entries in use.
All inputs are finite; a program needn't handle non-finite values.
Results may differ from the reference program's by a relative error of at most 0.0003.
Values sent between devices are 32-bit elements; how exact they have to be, the bound alone decides.
A program may use at most 192 MiB of HBM per device.

```python
import math
import jax
import jax.numpy as jnp
from jax import lax

V_LEN = 32768
BU = 64
FACET = 128
CH_DEV = 2
CH = 8
TPD = 4
TV = 1024
TILES = 32
TLOC = 8
NW = 4
PER = 128
SENDERS = 32
TILE_CAP = 384
N_FFT = 8
N_CHAN = 4


def routing_tables(key):
    base_key = jax.random.fold_in(key, 4242)
    key_list = jax.random.split(base_key, 5)
    slot_total = SENDERS * PER
    counts = jax.random.randint(key_list[0], (SENDERS, SENDERS), 3 * PER // 4, PER + 1)
    full_source = jax.random.randint(key_list[1], (SENDERS,), 0, SENDERS)
    counts = jnp.where(jnp.arange(SENDERS, dtype=jnp.int32)[:, None] == full_source[None, :], PER, counts)
    slot_ids = jnp.arange(slot_total, dtype=jnp.int32)
    usable = slot_ids[None, :] % PER < jnp.repeat(counts.T, PER, axis=1)
    ranks = jax.vmap(lambda one_key: jax.random.permutation(one_key, slot_total))(jax.random.split(key_list[2], SENDERS))
    ranks = ranks.astype(jnp.int32)
    scores = jnp.where(usable, ranks, ranks + slot_total)
    ordering = jnp.argsort(scores, axis=1, stable=True).astype(jnp.int32)
    loads = jax.random.randint(key_list[3], (SENDERS, TLOC), TILE_CAP // 2, TILE_CAP + 1)
    heavy = jax.random.randint(key_list[4], (SENDERS,), 0, TLOC)
    loads = jnp.where(jnp.arange(TLOC, dtype=jnp.int32)[None, :] == heavy[:, None], TILE_CAP, loads)
    starts = jnp.cumsum(loads, axis=1) - loads
    picks = (starts[:, :, None] + jnp.arange(TILE_CAP, dtype=jnp.int32)[None, None, :]) % slot_total
    lists = jnp.take_along_axis(ordering, picks.reshape(SENDERS, TLOC * TILE_CAP), axis=1)
    lists = lists.reshape(SENDERS, TLOC, TILE_CAP).astype(jnp.int32)
    return (counts.astype(jnp.int32), lists, loads.astype(jnp.int32))


def draw_send_counts(key, part):
    return routing_tables(key)[0]


def draw_tile_lists(key, part):
    return routing_tables(key)[1]


def draw_tile_counts(key, part):
    return routing_tables(key)[2]


def set_ends(entries, stream_key, low, high):
    longest = entries.shape.index(max(entries.shape))
    spots = []
    for shift in (0, 1):
        where = [jax.random.randint(jax.random.fold_in(stream_key, axis), (), 0, length) for axis, length in enumerate(entries.shape)]
        where[longest] = (where[longest] + shift) % entries.shape[longest]
        spots.append(tuple(where))
    return entries.at[spots[0]].set(low).at[spots[1]].set(high)


def block_levels(key, dims, cuts, low, top_value):
    level = 1.0
    for axis_at, shards_of in cuts:
        heights = jax.random.uniform(jax.random.fold_in(jax.random.fold_in(key, 6), axis_at), (shards_of,), jnp.float32, low / len(cuts), top_value / len(cuts))
        level = level * jnp.repeat(jnp.exp(heights), dims[axis_at] // shards_of).reshape((-1,) + (1,) * (len(dims) - 1 - axis_at))
    return level


def centred(rng, dims, scale, reach, cuts=(), held_as=jnp.bfloat16):
    drawn = jax.random.normal(rng, dims, jnp.float32) * scale
    if len(cuts) > 0:
        drawn = block_levels(rng, dims, cuts, -0.22, 0.18) * drawn
    return jnp.clip(drawn, min=-reach, max=reach).astype(held_as)


def setup_inputs(seed: int = 0) -> dict:
    key_of = jax.random.split(jax.random.key(seed), 11)
    return {
        "visibilities": centred(key_of[0], (SENDERS, 2, SENDERS, PER), 1.0, 6.0, ((0, 32),), jnp.float32),
        "positions": jnp.clip(1.0 * jax.random.uniform(key_of[1], (SENDERS, 2, SENDERS, PER), jnp.float32) ** block_levels(key_of[1], (SENDERS, 2, SENDERS, PER), ((0, 32),), -0.2, 0.2), 0.0, 1.0),
        "cell_row": set_ends(jax.random.randint(key_of[2], (SENDERS, SENDERS, PER), NW, BU - NW), jax.random.fold_in(key_of[2], 1), NW, (BU - NW) - 1).astype(jnp.int32),
        "cell_column": set_ends(jax.random.randint(key_of[3], (SENDERS, SENDERS, PER), NW, TV - NW), jax.random.fold_in(key_of[3], 1), NW, (TV - NW) - 1).astype(jnp.int32),
        "kernel_class": set_ends(jax.random.randint(key_of[4], (SENDERS, SENDERS, PER), 0, NW), jax.random.fold_in(key_of[4], 1), 0, NW - 1).astype(jnp.int32),
        "send_counts": draw_send_counts(jax.random.fold_in(key_of[10], 71), 0),
        "tile_lists": draw_tile_lists(jax.random.fold_in(key_of[10], 71), 0),
        "tile_counts": draw_tile_counts(jax.random.fold_in(key_of[10], 71), 0),
        "model_image": centred(key_of[8], (CH, FACET, V_LEN), 1.0, 6.0, ((0, 4), (1, 8)), jnp.float32),
        "threshold": jnp.clip(jnp.exp(math.log(3.0) - 1.7917595 * jax.random.uniform(key_of[9], (CH,), jnp.float32) ** block_levels(key_of[9], (CH,), ((0, 4),), -0.2, 0.2)), 0.5, 3.0),
    }


LOOP_GAIN = 0.7
EXACT_ARITHMETIC = lax.Precision.HIGHEST

def kernel_table(center_cell, fraction, class_index, length):
    grid_cells = jnp.arange(length, dtype=jnp.int32)
    distance = grid_cells[None, :] - center_cell[:, None]
    half_width = class_index + 1
    inside = jnp.abs(distance) <= half_width[:, None]
    spread = 0.6 * half_width.astype(jnp.float32)
    offset = distance.astype(jnp.float32) - fraction[:, None]
    shape_value = jnp.exp(-offset * offset / (2.0 * spread[:, None] * spread[:, None]))
    return jnp.where(inside, shape_value, jnp.zeros_like(shape_value))

def band_phases(band_rows, image_rows, grid_side):
    row_index = jnp.arange(band_rows, dtype=jnp.int32)
    image_index = jnp.arange(image_rows, dtype=jnp.int32)
    phase_index = (grid_side // 2 + row_index)[None, :] * image_index[:, None] % image_rows
    angle = -2.0 * math.pi / image_rows * phase_index.astype(jnp.float32)
    return (jnp.cos(angle), jnp.sin(angle))

def listed_entries(dest, visibilities, positions, cell_row, cell_column, kernel_class, tile_lists, tile_counts):
    slot_lists = tile_lists[dest]
    source = slot_lists // PER
    slot_index = slot_lists % PER
    listed = (jnp.arange(TILE_CAP, dtype=jnp.int32)[None, :] < tile_counts[dest][:, None]).astype(jnp.float32)
    values = visibilities[source, :, dest, slot_index]
    fraction = positions[source, :, dest, slot_index]
    classes = kernel_class[source, dest, slot_index].reshape(-1)
    row_kernel = kernel_table(cell_row[source, dest, slot_index].reshape(-1), fraction[..., 0].reshape(-1), classes, BU)
    column_kernel = kernel_table(cell_column[source, dest, slot_index].reshape(-1), fraction[..., 1].reshape(-1), classes, TV)
    row_kernel = row_kernel.reshape(TLOC, TILE_CAP, BU)
    column_kernel = column_kernel.reshape(TLOC, TILE_CAP, TV)
    return (source, slot_index, listed, values, row_kernel, column_kernel)

def reference(visibilities, positions, cell_row, cell_column, kernel_class, send_counts, tile_lists, tile_counts, model_image, threshold):
    dirty_scale = 1.0 / math.sqrt(TILES * TILE_CAP)
    back_scale = 0.5 / math.sqrt(FACET * V_LEN)

    def grid_device(dest):
        source, slot_index, listed, values, row_kernel, column_kernel = listed_entries(dest, visibilities, positions, cell_row, cell_column, kernel_class, tile_lists, tile_counts)
        weights = jnp.moveaxis(values, 2, 0) * listed[None]
        weighted = row_kernel[None] * weights[..., None]
        return jnp.einsum('ctku,tkv->ctuv', weighted, column_kernel, precision=EXACT_ARITHMETIC)
    tiles = lax.map(grid_device, jnp.arange(SENDERS, dtype=jnp.int32))
    channel_grid = tiles.reshape(N_FFT, N_CHAN, 2, CH_DEV, TPD, BU, TV).transpose(2, 1, 3, 5, 0, 4, 6)
    channel_grid = channel_grid.reshape(2, CH, BU, V_LEN)
    band_cos, band_sin = band_phases(BU, FACET, V_LEN)

    def image_channel(item):
        grid_re, grid_im, prior, clip_level = item
        spectrum = jnp.fft.fft(grid_re + 1j * grid_im, axis=1)
        spec_re = jnp.real(spectrum)
        spec_im = jnp.imag(spectrum)
        dirty_image = (jnp.dot(band_cos, spec_re, precision=EXACT_ARITHMETIC) - jnp.dot(band_sin, spec_im, precision=EXACT_ARITHMETIC)) * dirty_scale
        updated = prior + LOOP_GAIN * (dirty_image - jnp.clip(dirty_image, -clip_level, clip_level))
        inverse = jnp.fft.ifft(updated, axis=1) * V_LEN
        inv_re = jnp.real(inverse)
        inv_im = jnp.imag(inverse)
        pred_re = (jnp.dot(band_cos.T, inv_re, precision=EXACT_ARITHMETIC) + jnp.dot(band_sin.T, inv_im, precision=EXACT_ARITHMETIC)) * back_scale
        pred_im = (jnp.dot(band_cos.T, inv_im, precision=EXACT_ARITHMETIC) - jnp.dot(band_sin.T, inv_re, precision=EXACT_ARITHMETIC)) * back_scale
        return (updated, jnp.stack([pred_re, pred_im]))
    updated_model, predicted = lax.map(image_channel, (channel_grid[0], channel_grid[1], model_image, threshold))
    predicted = predicted.transpose(1, 0, 2, 3).reshape(2, N_CHAN, CH_DEV, BU, N_FFT, TPD, TV)
    tile_grids = predicted.transpose(4, 1, 0, 2, 5, 3, 6).reshape(SENDERS, 2, TLOC, BU, TV)

    def degrid_device(item):
        dest, grids = item
        source, slot_index, listed, values, row_kernel, column_kernel = listed_entries(dest, visibilities, positions, cell_row, cell_column, kernel_class, tile_lists, tile_counts)
        partial_value = jnp.einsum('tku,ctuv->ctkv', row_kernel, grids, precision=EXACT_ARITHMETIC)
        predicted_slot = lax.optimization_barrier(jnp.sum(partial_value * column_kernel[None], axis=3)) * listed[None]
        received = jnp.zeros((2, SENDERS, PER), jnp.float32)
        return received.at[:, source, slot_index].add(predicted_slot)
    returned = lax.map(degrid_device, (jnp.arange(SENDERS, dtype=jnp.int32), tile_grids))
    returned = returned.transpose(2, 1, 0, 3)
    sent_live = jnp.arange(PER, dtype=jnp.int32)[None, None, :] < send_counts[:, :, None]
    residuals = jnp.where(sent_live[:, None], visibilities - returned, jnp.zeros_like(visibilities))
    return (updated_model, residuals)
```

```python
import functools
import math

import jax
import jax.numpy as jnp
import ml_dtypes
import numpy as np
from jax import lax
from jax.experimental import pallas as pl
from jax.experimental.pallas import tpu as pltpu
from jax.sharding import PartitionSpec as P

BU = 64
LOOP_GAIN = 0.7
LANES = 128
GROUPS = 8
SPAN = GROUPS * LANES
REACH = 144
VMEM_BYTES = 56 * 1024 * 1024
F32 = jnp.float32
BF16 = jnp.bfloat16
NN = (((1,), (0,)), ((), ()))
NT = (((1,), (1,)), ((), ()))


def split_table(table):
    table = np.asarray(table, np.float32)
    high = table.astype(ml_dtypes.bfloat16)
    low = (table - high.astype(np.float32)).astype(ml_dtypes.bfloat16)
    return np.stack([high, low])


def split(value):
    high = value.astype(BF16)
    low = (value - high.astype(F32)).astype(BF16)
    return high, low


def dot(a, b, dims):
    return lax.dot_general(a, b, dims, preferred_element_type=F32)


def dot3(a, b, dims):
    return dot(a[0], b[0], dims) + (dot(a[0], b[1], dims) + dot(a[1], b[0], dims))


def unit(product, modulus):
    angle = 2.0 * np.pi / modulus * (product % modulus)
    return np.cos(angle), np.sin(angle)


def transform_tables(grid_side):
    lead = grid_side // LANES
    long_index, short_index = np.arange(lead), np.arange(LANES)
    cos1, sin1 = unit(long_index[:, None] * long_index[None, :], lead)
    cos2, sin2 = unit(short_index[:, None] * short_index[None, :], LANES)
    twist_cos, twist_sin = unit(long_index[:, None] * short_index[None, :], grid_side)
    first = np.block([[cos1, sin1], [-sin1, cos1]])
    second = np.concatenate([cos2, sin2], axis=1)
    third = np.concatenate([cos2, sin2], axis=0)
    last = np.block([[cos1, -sin1], [sin1, cos1]])
    return (
        split_table(first),
        split_table(second),
        split_table(third),
        split_table(last),
        np.stack([twist_cos, twist_sin]).astype(np.float32),
        np.stack([twist_cos.T, twist_sin.T]).astype(np.float32),
    )


def gather_kernel(senders, width, data_ref, slot_ref, live_ref, out_ref, table_ref):
    padded = table_ref.shape[1]
    data = data_ref[...]
    high = data.astype(BF16).astype(F32)
    rest = data - high
    middle = rest.astype(BF16).astype(F32)
    low = (rest - middle).astype(BF16).astype(F32)
    parts = [high, middle, low]
    if padded > 3 * senders:
        parts.append(jnp.zeros((padded - 3 * senders, data.shape[1]), F32))
    table_ref[...] = jnp.concatenate(parts, axis=0).T.astype(BF16)
    lists, _, cap = slot_ref.shape
    pieces = cap // width

    def step(index, carry):
        k = index // pieces
        at = pl.multiple_of(lax.rem(index, pieces) * width, LANES)
        slots = slot_ref[k, :, pl.ds(at, width)]
        live = live_ref[k, :, pl.ds(at, width)]
        source = slots // LANES
        place = slots - source * LANES
        sender = lax.broadcasted_iota(jnp.int32, (senders, width), 0)
        chosen = jnp.where(sender == source, 1.0, 0.0).astype(F32)
        picks = [chosen] * 3
        if padded > 3 * senders:
            picks.append(jnp.zeros((padded - 3 * senders, width), F32))
        picked = dot(table_ref[...], jnp.concatenate(picks, axis=0).astype(BF16), NN)
        here = lax.broadcasted_iota(jnp.int32, (LANES, width), 0) == place
        rows = []
        for part in range(7):
            block = picked[part * LANES : (part + 1) * LANES]
            rows.append(jnp.sum(jnp.where(here, block, 0.0), axis=0, keepdims=True))
        rows[0] = rows[0] * live
        rows[1] = rows[1] * live
        rows.append(live)
        out_ref[k, :, pl.ds(at, width)] = jnp.concatenate(rows, axis=0)
        return carry

    lax.fori_loop(0, lists * pieces, step, 0)


def scatter_kernel(senders, width, value_ref, slot_ref, live_ref, out_ref):
    lists, _, cap = slot_ref.shape
    pieces = cap // width
    out_ref[...] = jnp.zeros_like(out_ref)

    def step(index, carry):
        k = index // pieces
        at = pl.multiple_of(lax.rem(index, pieces) * width, LANES)
        slots = slot_ref[k, :, pl.ds(at, width)]
        live = live_ref[k, :, pl.ds(at, width)]
        values = value_ref[k, :, pl.ds(at, width)] * live
        source = slots // LANES
        place = slots - source * LANES
        sender = lax.broadcasted_iota(jnp.int32, (senders, width), 0)
        chosen = jnp.where(sender == source, 1.0, 0.0).astype(BF16)
        here = lax.broadcasted_iota(jnp.int32, (LANES, width), 0) == place
        spread = jnp.concatenate(
            [jnp.where(here, values[part : part + 1], 0.0) for part in range(2)], axis=0
        )
        high, low = split(spread)
        out_ref[...] += dot(chosen, high, NT) + dot(chosen, low, NT)
        return carry

    lax.fori_loop(0, lists * pieces, step, 0)


def cycle_kernel(
    plan,
    entry_ref,
    band_ref,
    model_ref,
    threshold_ref,
    first_ref,
    second_ref,
    third_ref,
    last_ref,
    twist_ref,
    twist_t_ref,
    updated_ref,
    predicted_ref,
    grid_ref,
    row_ref,
):
    (row_local, tiles_each, tile_cols, width, group, dirty_scale, back_scale) = plan
    owners, lists, _, cap = entry_ref.shape
    rows_total, lead2, _ = grid_ref.shape
    lead = lead2 // 2
    pieces = cap // width
    steps = owners * lists * pieces
    gathered = tile_cols < SPAN or pieces > 1

    def locate(index):
        piece = lax.rem(index, pieces)
        listing = index // pieces
        owner = listing // lists
        k = lax.rem(listing, lists)
        channel = k // tiles_each
        column = (owner * tiles_each + lax.rem(k, tiles_each)) * tile_cols
        span = column // SPAN
        inner = column - span * SPAN
        at = pl.multiple_of(piece * width, LANES)
        return owner, k, at, channel, span, inner

    def column_table(entries, inner):
        column = entries[5:6] + inner.astype(F32)
        half_width = entries[6:7] + 1.0
        rate = -1.0 / (0.72 * half_width * half_width)
        home = jnp.floor((column - 4.0) * (1.0 / LANES))
        local = column - home * LANES
        place = lax.broadcasted_iota(jnp.int32, (REACH, width), 0).astype(F32)
        distance = place - local
        offset = distance - entries[3:4]
        shape_value = jnp.exp(offset * offset * rate)
        table = jnp.where(jnp.abs(distance) <= half_width, shape_value, 0.0)
        high, low = split(table)
        rest = jnp.zeros((2 * LANES - REACH, width), BF16)
        high = jnp.concatenate([high, rest], axis=0)
        low = jnp.concatenate([low, rest], axis=0)
        which = lax.broadcasted_iota(jnp.int32, (GROUPS, width), 0).astype(F32)
        return (high, low), jnp.where(which == home, 1.0, 0.0)

    if gathered:
        grid_ref[...] = jnp.zeros_like(grid_ref)

    def grid_step(index, carry):
        owner, k, at, channel, span, inner = locate(index)
        entries = entry_ref[owner, k, :, pl.ds(at, width)]
        half_width = entries[6:7] + 1.0
        rate = -1.0 / (0.72 * half_width * half_width)
        band_row = lax.broadcasted_iota(jnp.int32, (BU, width), 0).astype(F32)
        distance = band_row - entries[4:5]
        offset = distance - entries[2:3]
        row_kernel = jnp.where(
            jnp.abs(distance) <= half_width, jnp.exp(offset * offset * rate), 0.0
        )
        phased = dot3((band_ref[0], band_ref[1]), split(row_kernel), NN)
        row_ref[index] = phased
        phased_re, phased_im = phased[:row_local], phased[row_local:]
        weight_re = entries[0:1] * phased_re - entries[1:2] * phased_im
        weight_im = entries[0:1] * phased_im + entries[1:2] * phased_re
        table, home = column_table(entries, inner)
        spread = jnp.concatenate(
            [
                jnp.broadcast_to(weight[i : i + 1], (GROUPS, width)) * home
                for weight in (weight_re, weight_im)
                for i in range(row_local)
            ],
            axis=0,
        )
        wide = dot3(split(spread), table, NT)
        block = wide[:, :LANES] + pltpu.roll(wide[:, LANES:], 1, 0)
        block = block.reshape(2, row_local, GROUPS, LANES)
        first_row = pl.multiple_of(channel * row_local, row_local)
        for part in range(2):
            spot = (
                pl.ds(first_row, row_local),
                pl.ds(pl.multiple_of(part * lead + span * GROUPS, GROUPS), GROUPS),
            )
            if gathered:
                grid_ref[spot] += block[part]
            else:
                grid_ref[spot] = block[part]
        return carry

    lax.fori_loop(0, steps, grid_step, 0)

    def image_step(index, carry):
        first_row = index * 2
        cos, sin = twist_ref[0], twist_ref[1]
        columns = jnp.concatenate([grid_ref[first_row], grid_ref[first_row + 1]], axis=1)
        stage = dot3((first_ref[0], first_ref[1]), split(columns), NN)
        cos_t, sin_t = twist_t_ref[0], twist_t_ref[1]
        turned_back = []
        for lane in range(2):
            row = first_row + lane
            real = stage[:lead, lane * LANES : (lane + 1) * LANES]
            imag = stage[lead:, lane * LANES : (lane + 1) * LANES]
            turned = jnp.concatenate([real * cos + imag * sin, imag * cos - real * sin], axis=1)
            dirty = dot3((second_ref[0], second_ref[1]), split(turned), NT) * dirty_scale
            level = threshold_ref[row // row_local]
            change = LOOP_GAIN * (dirty - jnp.clip(dirty, -level, level))
            halves = []
            for half in range(lead // LANES):
                spot = (
                    row // group,
                    pl.ds(half * group + lax.rem(row, group), LANES, stride=(lead // LANES) * group),
                )
                updated = model_ref[spot] + change[:, half * LANES : (half + 1) * LANES]
                updated_ref[spot] = updated
                halves.append(updated)
            image = jnp.concatenate(halves, axis=1)
            back = dot3((third_ref[0], third_ref[1]), split(image), NN)
            real, imag = back[:LANES], back[LANES:]
            turned_back.append(
                jnp.concatenate(
                    [real * cos_t - imag * sin_t, real * sin_t + imag * cos_t], axis=1
                )
            )
        columns = dot3(
            (last_ref[0], last_ref[1]), split(jnp.concatenate(turned_back, axis=0)), NT
        )
        grid_ref[first_row] = columns[:, :LANES]
        grid_ref[first_row + 1] = columns[:, LANES:]
        return carry

    lax.fori_loop(0, rows_total // 2, image_step, 0)

    def degrid_step(index, carry):
        owner, k, at, channel, span, inner = locate(index)
        entries = entry_ref[owner, k, :, pl.ds(at, width)]
        table, home = column_table(entries, inner)
        first_row = pl.multiple_of(channel * row_local, row_local)
        blocks = []
        for part in range(2):
            block = grid_ref[
                pl.ds(first_row, row_local),
                pl.ds(pl.multiple_of(part * lead + span * GROUPS, GROUPS), GROUPS),
            ]
            blocks.append(block.reshape(row_local * GROUPS, LANES))
        block = jnp.concatenate(blocks, axis=0)
        wide = jnp.concatenate([block, pltpu.roll(block, block.shape[0] - 1, 0)], axis=1)
        sampled = dot3(split(wide), table, NN)
        phased = row_ref[index]
        total_re = jnp.zeros((GROUPS, width), F32)
        total_im = jnp.zeros((GROUPS, width), F32)
        for i in range(row_local):
            real = sampled[i * GROUPS : (i + 1) * GROUPS]
            imag = sampled[(row_local + i) * GROUPS : (row_local + i + 1) * GROUPS]
            turn_re = phased[i : i + 1]
            turn_im = phased[row_local + i : row_local + i + 1]
            total_re += turn_re * real + turn_im * imag
            total_im += turn_re * imag - turn_im * real
        predicted_ref[owner, k, :, pl.ds(at, width)] = jnp.concatenate(
            [
                jnp.sum(total_re * home, axis=0, keepdims=True) * back_scale,
                jnp.sum(total_im * home, axis=0, keepdims=True) * back_scale,
            ],
            axis=0,
        )
        return carry

    lax.fori_loop(0, steps, degrid_step, 0)


def vmem(count):
    return [pl.BlockSpec(memory_space=pltpu.VMEM)] * count


def params():
    return pltpu.CompilerParams(vmem_limit_bytes=VMEM_BYTES)


def gather_entries(received, slots, live, width):
    senders = received.shape[0]
    padded = -(-3 * senders // LANES) * LANES
    lists, _, cap = slots.shape
    return pl.pallas_call(
        functools.partial(gather_kernel, senders, width),
        out_shape=jax.ShapeDtypeStruct((lists, 8, cap), F32),
        in_specs=vmem(3),
        out_specs=vmem(1)[0],
        scratch_shapes=[pltpu.VMEM((received.shape[1], padded), BF16)],
        compiler_params=params(),
        name="gather_entries",
    )(received, slots, live)


def scatter_values(values, slots, live, senders, width):
    return pl.pallas_call(
        functools.partial(scatter_kernel, senders, width),
        out_shape=jax.ShapeDtypeStruct((senders, 2 * LANES), F32),
        in_specs=vmem(3),
        out_specs=vmem(1)[0],
        compiler_params=params(),
        name="scatter_values",
    )(values, slots, live)


def imaging_cycle(entries, band, model, threshold, plan, grid_side):
    owners, lists, _, cap = entries.shape
    row_local, _, _, width, group = plan[:5]
    lead = grid_side // LANES
    rows_total = model.shape[0] * group
    steps = owners * lists * (cap // width)
    tables = transform_tables(grid_side)
    return pl.pallas_call(
        functools.partial(cycle_kernel, plan),
        out_shape=(
            jax.ShapeDtypeStruct(model.shape, F32),
            jax.ShapeDtypeStruct((owners, lists, 2, cap), F32),
        ),
        in_specs=vmem(3) + [pl.BlockSpec(memory_space=pltpu.SMEM)] + vmem(6),
        out_specs=tuple(vmem(2)),
        scratch_shapes=[
            pltpu.VMEM((rows_total, 2 * lead, LANES), F32),
            pltpu.VMEM((steps, 2 * row_local, width), F32),
        ],
        compiler_params=params(),
        name="imaging_cycle",
    )(entries, band, model, threshold, *[jnp.asarray(table) for table in tables])


def per_device(
    visibilities,
    positions,
    cell_row,
    cell_column,
    kernel_class,
    send_counts,
    tile_lists,
    tile_counts,
    model_image,
    threshold,
):
    fft_devices = lax.axis_size("fft")
    chan_devices = lax.axis_size("chan")
    senders = fft_devices * chan_devices
    per_pair = visibilities.shape[3]
    local_tiles = tile_lists.shape[1]
    tile_cap = tile_lists.shape[2]
    chan_local, row_local, grid_side = model_image.shape
    tiles_each = local_tiles // chan_local
    facet_rows = row_local * fft_devices
    tile_cols = grid_side // (fft_devices * tiles_each)
    dirty_scale = 1.0 / math.sqrt(fft_devices * tiles_each * tile_cap)
    back_scale = 0.5 / math.sqrt(facet_rows * grid_side)
    width = 384 if tile_cap % 384 == 0 else LANES
    group = math.gcd(row_local, 8)

    labels = jnp.stack([cell_row, cell_column, kernel_class], axis=1).astype(F32)
    payload = jnp.concatenate([visibilities, positions, labels], axis=1)[0]
    payload = payload.transpose(1, 0, 2).reshape(senders, 7 * per_pair)
    received = lax.all_to_all(payload, ("fft", "chan"), split_axis=0, concat_axis=0, tiled=True)
    slots = tile_lists[0][:, None, :]
    live = jnp.arange(tile_cap, dtype=jnp.int32)[None, :] < tile_counts[0][:, None]
    live = live.astype(F32)[:, None, :]
    entries = gather_entries(received, slots, live, width)
    entries = lax.all_gather(entries, "fft", axis=0, tiled=False)

    band_index = np.arange(facet_rows)[:, None] * (grid_side // 2 + np.arange(BU))[None, :]
    band_cos, band_sin = unit(band_index, facet_rows)
    band = np.stack([band_cos, -band_sin]).reshape(2, fft_devices, row_local, BU)
    band = split_table(band.transpose(1, 0, 2, 3).reshape(fft_devices, 2 * row_local, BU))
    band = lax.dynamic_index_in_dim(
        jnp.asarray(band), lax.axis_index("fft"), axis=1, keepdims=False
    )
    lanes_total = grid_side // LANES
    rows_total = chan_local * row_local
    model = model_image.reshape(rows_total // group, group, lanes_total, LANES)
    model = model.transpose(0, 2, 1, 3).reshape(rows_total // group, lanes_total * group, LANES)
    plan = (row_local, tiles_each, tile_cols, width, group, dirty_scale, back_scale)
    updated, partial = imaging_cycle(entries, band, model, threshold, plan, grid_side)
    updated = updated.reshape(rows_total // group, lanes_total, group, LANES)
    updated = updated.transpose(0, 2, 1, 3).reshape(model_image.shape)

    partial = lax.all_to_all(partial, "fft", split_axis=0, concat_axis=0, tiled=True)
    predicted = jnp.sum(partial, axis=0)
    outgoing = scatter_values(predicted, slots, live, senders, width)
    returned = lax.all_to_all(outgoing, ("fft", "chan"), split_axis=0, concat_axis=0, tiled=True)
    returned = returned.reshape(senders, 2, per_pair).transpose(1, 0, 2)[None]
    sent_live = jnp.arange(per_pair, dtype=jnp.int32)[None, None, :] < send_counts[0][None, :, None]
    residuals = jnp.where(sent_live[:, None], visibilities - returned, jnp.zeros_like(visibilities))
    return (updated, residuals)


def solution(mesh):
    placed = (
        P(("fft", "chan"), None, None, None),
        P(("fft", "chan"), None, None, None),
        P(("fft", "chan"), None, None),
        P(("fft", "chan"), None, None),
        P(("fft", "chan"), None, None),
        P(("fft", "chan"), None),
        P(("fft", "chan"), None, None),
        P(("fft", "chan"), None),
        P("chan", "fft", None),
        P("chan"),
    )
    return jax.shard_map(
        per_device,
        mesh=mesh,
        in_specs=placed,
        out_specs=(P("chan", "fft", None), P(("fft", "chan"), None, None, None)),
        check_vma=False,
    )
```

```python
import functools
import math

import jax
import jax.numpy as jnp
import ml_dtypes
import numpy as np
from jax import lax
from jax.experimental import pallas as pl
from jax.experimental.pallas import tpu as pltpu
from jax.sharding import PartitionSpec as P

BU = 64
LOOP_GAIN = 0.7
LANES = 128
GROUPS = 8
SPAN = GROUPS * LANES
REACH = 144
VMEM_BYTES = 56 * 1024 * 1024
F32 = jnp.float32
BF16 = jnp.bfloat16
NN = (((1,), (0,)), ((), ()))
NT = (((1,), (1,)), ((), ()))


def split_table(table):
    table = np.asarray(table, np.float32)
    high = table.astype(ml_dtypes.bfloat16)
    low = (table - high.astype(np.float32)).astype(ml_dtypes.bfloat16)
    return high, low


def table3(table):
    high, low = split_table(table)
    return np.concatenate([high, high, low], axis=-1)


def split(value):
    high = value.astype(BF16)
    low = (value - high.astype(F32)).astype(BF16)
    return high, low


def dot(a, b, dims):
    return lax.dot_general(a, b, dims, preferred_element_type=F32)


def side3(value, axis):
    high, low = split(value)
    return jnp.concatenate([high, low, high], axis=axis)


def unit(product, modulus):
    angle = 2.0 * np.pi / modulus * (product % modulus)
    return np.cos(angle), np.sin(angle)


def transform_tables(grid_side):
    lead = grid_side // LANES
    long_index, short_index = np.arange(lead), np.arange(LANES)
    cos1, sin1 = unit(long_index[:, None] * long_index[None, :], lead)
    cos2, sin2 = unit(short_index[:, None] * short_index[None, :], LANES)
    twist_cos, twist_sin = unit(long_index[:, None] * short_index[None, :], grid_side)
    first = np.block([[cos1, sin1], [-sin1, cos1]])
    second = np.concatenate([cos2, sin2], axis=1)
    third = np.concatenate([cos2, sin2], axis=0)
    last = np.block([[cos1, -sin1], [sin1, cos1]])
    return (
        table3(first),
        table3(second),
        table3(third),
        table3(last),
        np.stack([twist_cos, twist_sin]).astype(np.float32),
        np.stack([twist_cos.T, twist_sin.T]).astype(np.float32),
    )


def gather_kernel(senders, width, data_ref, slot_ref, live_ref, out_ref, table_ref):
    padded = table_ref.shape[1]
    data = data_ref[...]
    high = data.astype(BF16).astype(F32)
    rest = data - high
    middle = rest.astype(BF16).astype(F32)
    low = (rest - middle).astype(BF16).astype(F32)
    parts = [high, middle, low]
    if padded > 3 * senders:
        parts.append(jnp.zeros((padded - 3 * senders, data.shape[1]), F32))
    table_ref[...] = jnp.concatenate(parts, axis=0).T.astype(BF16)
    lists, _, cap = slot_ref.shape
    pieces = cap // width

    def step(index, carry):
        k = index // pieces
        at = pl.multiple_of(lax.rem(index, pieces) * width, LANES)
        slots = slot_ref[k, :, pl.ds(at, width)]
        live = live_ref[k, :, pl.ds(at, width)]
        source = slots // LANES
        place = slots - source * LANES
        sender = lax.broadcasted_iota(jnp.int32, (senders, width), 0)
        chosen = jnp.where(sender == source, 1.0, 0.0).astype(F32)
        picks = [chosen] * 3
        if padded > 3 * senders:
            picks.append(jnp.zeros((padded - 3 * senders, width), F32))
        picked = dot(table_ref[...], jnp.concatenate(picks, axis=0).astype(BF16), NN)
        here = lax.broadcasted_iota(jnp.int32, (LANES, width), 0) == place
        rows = []
        for part in range(7):
            block = picked[part * LANES : (part + 1) * LANES]
            rows.append(jnp.sum(jnp.where(here, block, 0.0), axis=0, keepdims=True))
        rows[0] = rows[0] * live
        rows[1] = rows[1] * live
        rows.append(live)
        out_ref[k, :, pl.ds(at, width)] = jnp.concatenate(rows, axis=0)
        return carry

    lax.fori_loop(0, lists * pieces, step, 0)


def scatter_kernel(senders, width, value_ref, slot_ref, live_ref, out_ref):
    lists, _, cap = slot_ref.shape
    pieces = cap // width
    out_ref[...] = jnp.zeros_like(out_ref)

    def step(index, carry):
        k = index // pieces
        at = pl.multiple_of(lax.rem(index, pieces) * width, LANES)
        slots = slot_ref[k, :, pl.ds(at, width)]
        live = live_ref[k, :, pl.ds(at, width)]
        values = value_ref[k, :, pl.ds(at, width)] * live
        source = slots // LANES
        place = slots - source * LANES
        sender = lax.broadcasted_iota(jnp.int32, (senders, width), 0)
        chosen = jnp.where(sender == source, 1.0, 0.0).astype(BF16)
        here = lax.broadcasted_iota(jnp.int32, (LANES, width), 0) == place
        spread = jnp.concatenate(
            [jnp.where(here, values[part : part + 1], 0.0) for part in range(2)], axis=0
        )
        high, low = split(spread)
        out_ref[...] += dot(chosen, high, NT) + dot(chosen, low, NT)
        return carry

    lax.fori_loop(0, lists * pieces, step, 0)


def cycle_kernel(
    plan,
    entry_ref,
    band_ref,
    model_ref,
    threshold_ref,
    first_ref,
    second_ref,
    third_ref,
    last_ref,
    twist_ref,
    twist_t_ref,
    updated_ref,
    predicted_ref,
    grid_ref,
    row_ref,
):
    (row_local, tiles_each, tile_cols, width, group, dirty_scale, back_scale) = plan
    owners, lists, _, cap = entry_ref.shape
    rows_total, lead2, _ = grid_ref.shape
    lead = lead2 // 2
    pieces = cap // width
    steps = owners * lists * pieces
    gathered = tile_cols < SPAN or pieces > 1

    def locate(index):
        piece = lax.rem(index, pieces)
        listing = index // pieces
        owner = listing // lists
        k = lax.rem(listing, lists)
        channel = k // tiles_each
        column = (owner * tiles_each + lax.rem(k, tiles_each)) * tile_cols
        span = column // SPAN
        inner = column - span * SPAN
        at = pl.multiple_of(piece * width, LANES)
        return owner, k, at, channel, span, inner

    def column_table(entries, inner):
        column = entries[5:6] + inner.astype(F32)
        half_width = entries[6:7] + 1.0
        rate = -1.0 / (0.72 * half_width * half_width)
        home = jnp.floor((column - 4.0) * (1.0 / LANES))
        local = column - home * LANES
        place = lax.broadcasted_iota(jnp.int32, (REACH, width), 0).astype(F32)
        distance = place - local
        offset = distance - entries[3:4]
        shape_value = jnp.exp(offset * offset * rate)
        table = jnp.where(jnp.abs(distance) <= half_width, shape_value, 0.0)
        high, low = split(table)
        rest = jnp.zeros((2 * LANES - REACH, width), BF16)
        which = lax.broadcasted_iota(jnp.int32, (GROUPS, width), 0).astype(F32)
        return high, low, rest, jnp.where(which == home, 1.0, 0.0)

    if gathered:
        grid_ref[...] = jnp.zeros_like(grid_ref)

    def grid_step(index, carry):
        owner, k, at, channel, span, inner = locate(index)
        entries = entry_ref[owner, k, :, pl.ds(at, width)]
        half_width = entries[6:7] + 1.0
        rate = -1.0 / (0.72 * half_width * half_width)
        band_row = lax.broadcasted_iota(jnp.int32, (BU, width), 0).astype(F32)
        distance = band_row - entries[4:5]
        offset = distance - entries[2:3]
        row_kernel = jnp.where(
            jnp.abs(distance) <= half_width, jnp.exp(offset * offset * rate), 0.0
        )
        phased = dot(band_ref[...], side3(row_kernel, 0), NN)
        row_ref[index] = phased
        phased_re, phased_im = phased[:row_local], phased[row_local:]
        weight_re = entries[0:1] * phased_re - entries[1:2] * phased_im
        weight_im = entries[0:1] * phased_im + entries[1:2] * phased_re
        high, low, rest, home = column_table(entries, inner)
        table = jnp.concatenate(
            [
                jnp.concatenate([high, low, high], axis=1),
                jnp.concatenate([rest, rest, rest], axis=1),
            ],
            axis=0,
        )
        spread = jnp.concatenate(
            [
                jnp.broadcast_to(weight[i : i + 1], (GROUPS, width)) * home
                for weight in (weight_re, weight_im)
                for i in range(row_local)
            ],
            axis=0,
        )
        spread_high, spread_low = split(spread)
        spread = jnp.concatenate([spread_high, spread_high, spread_low], axis=1)
        wide = dot(spread, table, NT)
        block = wide[:, :LANES] + pltpu.roll(wide[:, LANES:], 1, 0)
        block = block.reshape(2, row_local, GROUPS, LANES)
        first_row = pl.multiple_of(channel * row_local, row_local)
        for part in range(2):
            spot = (
                pl.ds(first_row, row_local),
                pl.ds(pl.multiple_of(part * lead + span * GROUPS, GROUPS), GROUPS),
            )
            if gathered:
                grid_ref[spot] += block[part]
            else:
                grid_ref[spot] = block[part]
        return carry

    lax.fori_loop(0, steps, grid_step, 0, unroll=2)

    together = math.gcd(rows_total, 4)

    def image_step(index, carry):
        first_row = index * together
        cos, sin = twist_ref[0], twist_ref[1]
        cos_t, sin_t = twist_t_ref[0], twist_t_ref[1]
        columns = jnp.concatenate(
            [grid_ref[first_row + lane] for lane in range(together)], axis=1
        )
        stage = dot(first_ref[...], side3(columns, 0), NN)
        turned_back = []
        for lane in range(together):
            row = first_row + lane
            real = stage[:lead, lane * LANES : (lane + 1) * LANES]
            imag = stage[lead:, lane * LANES : (lane + 1) * LANES]
            turned = jnp.concatenate([real * cos + imag * sin, imag * cos - real * sin], axis=1)
            dirty = dot(second_ref[...], side3(turned, 1), NT) * dirty_scale
            level = threshold_ref[row // row_local]
            change = LOOP_GAIN * (dirty - jnp.clip(dirty, -level, level))
            halves = []
            for half in range(lead // LANES):
                spot = (
                    row // group,
                    pl.ds(half * group + lax.rem(row, group), LANES, stride=(lead // LANES) * group),
                )
                updated = model_ref[spot] + change[:, half * LANES : (half + 1) * LANES]
                updated_ref[spot] = updated
                halves.append(updated)
            image = jnp.concatenate(halves, axis=1)
            back = dot(third_ref[...], side3(image, 0), NN)
            real, imag = back[:LANES], back[LANES:]
            turned_back.append(
                jnp.concatenate(
                    [real * cos_t - imag * sin_t, real * sin_t + imag * cos_t], axis=1
                )
            )
        columns = dot(last_ref[...], side3(jnp.concatenate(turned_back, axis=0), 1), NT)
        for lane in range(together):
            grid_ref[first_row + lane] = columns[:, lane * LANES : (lane + 1) * LANES]
        return carry

    lax.fori_loop(0, rows_total // together, image_step, 0)

    def degrid_step(index, carry):
        owner, k, at, channel, span, inner = locate(index)
        entries = entry_ref[owner, k, :, pl.ds(at, width)]
        high, low, rest, home = column_table(entries, inner)
        table = jnp.concatenate([high, rest, low, rest, high, rest], axis=0)
        first_row = pl.multiple_of(channel * row_local, row_local)
        blocks = []
        for part in range(2):
            block = grid_ref[
                pl.ds(first_row, row_local),
                pl.ds(pl.multiple_of(part * lead + span * GROUPS, GROUPS), GROUPS),
            ]
            blocks.append(block.reshape(row_local * GROUPS, LANES))
        block = jnp.concatenate(blocks, axis=0)
        wide = jnp.concatenate([block, pltpu.roll(block, block.shape[0] - 1, 0)], axis=1)
        wide_high, wide_low = split(wide)
        sampled = dot(jnp.concatenate([wide_high, wide_high, wide_low], axis=1), table, NN)
        phased = row_ref[index]
        total_re = jnp.zeros((GROUPS, width), F32)
        total_im = jnp.zeros((GROUPS, width), F32)
        for i in range(row_local):
            real = sampled[i * GROUPS : (i + 1) * GROUPS]
            imag = sampled[(row_local + i) * GROUPS : (row_local + i + 1) * GROUPS]
            turn_re = phased[i : i + 1]
            turn_im = phased[row_local + i : row_local + i + 1]
            total_re += turn_re * real + turn_im * imag
            total_im += turn_re * imag - turn_im * real
        predicted_ref[owner, k, :, pl.ds(at, width)] = jnp.concatenate(
            [
                jnp.sum(total_re * home, axis=0, keepdims=True) * back_scale,
                jnp.sum(total_im * home, axis=0, keepdims=True) * back_scale,
            ],
            axis=0,
        )
        return carry

    lax.fori_loop(0, steps, degrid_step, 0, unroll=2)


def vmem(count):
    return [pl.BlockSpec(memory_space=pltpu.VMEM)] * count


def params():
    return pltpu.CompilerParams(vmem_limit_bytes=VMEM_BYTES)


def gather_entries(received, slots, live, width):
    senders = received.shape[0]
    padded = -(-3 * senders // LANES) * LANES
    lists, _, cap = slots.shape
    return pl.pallas_call(
        functools.partial(gather_kernel, senders, width),
        out_shape=jax.ShapeDtypeStruct((lists, 8, cap), F32),
        in_specs=vmem(3),
        out_specs=vmem(1)[0],
        scratch_shapes=[pltpu.VMEM((received.shape[1], padded), BF16)],
        compiler_params=params(),
        name="gather_entries",
    )(received, slots, live)


def scatter_values(values, slots, live, senders, width):
    return pl.pallas_call(
        functools.partial(scatter_kernel, senders, width),
        out_shape=jax.ShapeDtypeStruct((senders, 2 * LANES), F32),
        in_specs=vmem(3),
        out_specs=vmem(1)[0],
        compiler_params=params(),
        name="scatter_values",
    )(values, slots, live)


def imaging_cycle(entries, band, model, threshold, plan, grid_side):
    owners, lists, _, cap = entries.shape
    row_local, _, _, width, group = plan[:5]
    lead = grid_side // LANES
    rows_total = model.shape[0] * group
    steps = owners * lists * (cap // width)
    tables = transform_tables(grid_side)
    return pl.pallas_call(
        functools.partial(cycle_kernel, plan),
        out_shape=(
            jax.ShapeDtypeStruct(model.shape, F32),
            jax.ShapeDtypeStruct((owners, lists, 2, cap), F32),
        ),
        in_specs=vmem(3) + [pl.BlockSpec(memory_space=pltpu.SMEM)] + vmem(6),
        out_specs=tuple(vmem(2)),
        scratch_shapes=[
            pltpu.VMEM((rows_total, 2 * lead, LANES), F32),
            pltpu.VMEM((steps, 2 * row_local, width), F32),
        ],
        compiler_params=params(),
        name="imaging_cycle",
    )(entries, band, model, threshold, *[jnp.asarray(table) for table in tables])


def per_device(
    visibilities,
    positions,
    cell_row,
    cell_column,
    kernel_class,
    send_counts,
    tile_lists,
    tile_counts,
    model_image,
    threshold,
):
    fft_devices = lax.axis_size("fft")
    chan_devices = lax.axis_size("chan")
    senders = fft_devices * chan_devices
    per_pair = visibilities.shape[3]
    local_tiles = tile_lists.shape[1]
    tile_cap = tile_lists.shape[2]
    chan_local, row_local, grid_side = model_image.shape
    tiles_each = local_tiles // chan_local
    facet_rows = row_local * fft_devices
    tile_cols = grid_side // (fft_devices * tiles_each)
    dirty_scale = 1.0 / math.sqrt(fft_devices * tiles_each * tile_cap)
    back_scale = 0.5 / math.sqrt(facet_rows * grid_side)
    width = 384 if tile_cap % 384 == 0 else LANES
    group = math.gcd(row_local, 8)

    labels = jnp.stack([cell_row, cell_column, kernel_class], axis=1).astype(F32)
    payload = jnp.concatenate([visibilities, positions, labels], axis=1)[0]
    payload = payload.transpose(1, 0, 2).reshape(senders, 7 * per_pair)
    received = lax.all_to_all(payload, ("fft", "chan"), split_axis=0, concat_axis=0, tiled=True)
    slots = tile_lists[0][:, None, :]
    live = jnp.arange(tile_cap, dtype=jnp.int32)[None, :] < tile_counts[0][:, None]
    live = live.astype(F32)[:, None, :]
    entries = gather_entries(received, slots, live, width)
    entries = lax.all_gather(entries, "fft", axis=0, tiled=False)

    band_index = np.arange(facet_rows)[:, None] * (grid_side // 2 + np.arange(BU))[None, :]
    band_cos, band_sin = unit(band_index, facet_rows)
    band = np.stack([band_cos, -band_sin]).reshape(2, fft_devices, row_local, BU)
    band = table3(band.transpose(1, 0, 2, 3).reshape(fft_devices, 2 * row_local, BU))
    band = lax.dynamic_index_in_dim(
        jnp.asarray(band), lax.axis_index("fft"), axis=0, keepdims=False
    )
    lanes_total = grid_side // LANES
    rows_total = chan_local * row_local
    model = model_image.reshape(rows_total // group, group, lanes_total, LANES)
    model = model.transpose(0, 2, 1, 3).reshape(rows_total // group, lanes_total * group, LANES)
    plan = (row_local, tiles_each, tile_cols, width, group, dirty_scale, back_scale)
    updated, partial = imaging_cycle(entries, band, model, threshold, plan, grid_side)
    updated = updated.reshape(rows_total // group, lanes_total, group, LANES)
    updated = updated.transpose(0, 2, 1, 3).reshape(model_image.shape)

    partial = lax.all_to_all(partial, "fft", split_axis=0, concat_axis=0, tiled=True)
    predicted = jnp.sum(partial, axis=0)
    outgoing = scatter_values(predicted, slots, live, senders, width)
    returned = lax.all_to_all(outgoing, ("fft", "chan"), split_axis=0, concat_axis=0, tiled=True)
    returned = returned.reshape(senders, 2, per_pair).transpose(1, 0, 2)[None]
    sent_live = jnp.arange(per_pair, dtype=jnp.int32)[None, None, :] < send_counts[0][None, :, None]
    residuals = jnp.where(sent_live[:, None], visibilities - returned, jnp.zeros_like(visibilities))
    return (updated, residuals)


def solution(mesh):
    placed = (
        P(("fft", "chan"), None, None, None),
        P(("fft", "chan"), None, None, None),
        P(("fft", "chan"), None, None),
        P(("fft", "chan"), None, None),
        P(("fft", "chan"), None, None),
        P(("fft", "chan"), None),
        P(("fft", "chan"), None, None),
        P(("fft", "chan"), None),
        P("chan", "fft", None),
        P("chan"),
    )
    return jax.shard_map(
        per_device,
        mesh=mesh,
        in_specs=placed,
        out_specs=(P("chan", "fft", None), P(("fft", "chan"), None, None, None)),
        check_vma=False,
    )
```

```python
import functools
import math

import jax
import jax.numpy as jnp
import ml_dtypes
import numpy as np
from jax import lax
from jax.experimental import pallas as pl
from jax.experimental.pallas import tpu as pltpu
from jax.sharding import PartitionSpec as P

BU = 64
LOOP_GAIN = 0.7
LANES = 128
GROUPS = 8
SPAN = GROUPS * LANES
REACH = 144
VMEM_BYTES = 56 * 1024 * 1024
F32 = jnp.float32
BF16 = jnp.bfloat16
NN = (((1,), (0,)), ((), ()))
NT = (((1,), (1,)), ((), ()))


def split_table(table):
    table = np.asarray(table, np.float32)
    high = table.astype(ml_dtypes.bfloat16)
    low = (table - high.astype(np.float32)).astype(ml_dtypes.bfloat16)
    return high, low


def table3(table):
    high, low = split_table(table)
    return np.concatenate([high, high, low], axis=-1)


def split(value):
    high = value.astype(BF16)
    low = (value - high.astype(F32)).astype(BF16)
    return high, low


def dot(a, b, dims):
    return lax.dot_general(a, b, dims, preferred_element_type=F32)


def side3(value, axis):
    high, low = split(value)
    return jnp.concatenate([high, low, high], axis=axis)


def unit(product, modulus):
    angle = 2.0 * np.pi / modulus * (product % modulus)
    return np.cos(angle), np.sin(angle)


def transform_tables(grid_side):
    lead = grid_side // LANES
    long_index, short_index = np.arange(lead), np.arange(LANES)
    cos1, sin1 = unit(long_index[:, None] * long_index[None, :], lead)
    cos2, sin2 = unit(short_index[:, None] * short_index[None, :], LANES)
    twist_cos, twist_sin = unit(long_index[:, None] * short_index[None, :], grid_side)
    first = np.block([[cos1, sin1], [-sin1, cos1]])
    second = np.concatenate([cos2, sin2], axis=1)
    third = np.concatenate([cos2, sin2], axis=0)
    last = np.block([[cos1, -sin1], [sin1, cos1]])
    return (
        table3(first),
        table3(second),
        table3(third),
        table3(last),
        np.stack([twist_cos, twist_sin]).astype(np.float32),
        np.stack([twist_cos.T, twist_sin.T]).astype(np.float32),
    )


def cycle_kernel(
    plan,
    payload_ref,
    slot_ref,
    live_ref,
    count_ref,
    band_ref,
    threshold_ref,
    second_ref,
    third_ref,
    twist_ref,
    twist_t_ref,
    first_any,
    last_any,
    model_any,
    updated_any,
    residual_ref,
    received_ref,
    table_ref,
    entry_ref,
    first_ref,
    last_ref,
    model_ref,
    updated_ref,
    grid_ref,
    row_ref,
    predicted_ref,
    arrived_ref,
    outgoing_ref,
    returned_ref,
    load_sem,
    payload_send,
    payload_recv,
    entry_send,
    entry_recv,
    partial_send,
    partial_recv,
    return_send,
    return_recv,
):
    (chan_devices, row_local, tiles_each, tile_cols, width, group, dirty_scale, back_scale) = plan
    owners, lists, _, cap = entry_ref.shape
    senders = owners * chan_devices
    rows_total, lead2, _ = grid_ref.shape
    lead = lead2 // 2
    pieces = cap // width
    rounds = lists * pieces
    gathered = tile_cols < SPAN or pieces > 1
    fft_at, chan_at = lax.axis_index("fft"), lax.axis_index("chan")
    me = fft_at * chan_devices + chan_at

    def place_of(device):
        return (device // chan_devices, lax.rem(device, chan_devices))

    def send(source, target, send_sem, recv_sem, device):
        return pltpu.make_async_remote_copy(
            src_ref=source,
            dst_ref=target,
            send_sem=send_sem,
            recv_sem=recv_sem,
            device_id=device,
            device_id_type=pl.DeviceIdType.MESH,
        )

    loads = [
        pltpu.make_async_copy(source, target, load_sem.at[i])
        for i, (source, target) in enumerate(
            ((model_any, model_ref), (first_any, first_ref), (last_any, last_ref))
        )
    ]
    for load in loads:
        load.start()

    barrier = pltpu.get_barrier_semaphore()
    for ahead in range(1, senders):
        pl.semaphore_signal(
            barrier,
            inc=1,
            device_id=place_of(lax.rem(me + ahead, senders)),
            device_id_type=pl.DeviceIdType.MESH,
        )
    pl.semaphore_wait(barrier, senders - 1)

    def payload_copy(ahead):
        target = lax.rem(me + ahead, senders)
        return send(
            payload_ref.at[target],
            received_ref.at[me],
            payload_send.at[ahead],
            payload_recv.at[ahead],
            place_of(target),
        )

    def payload_arrival(ahead):
        source = lax.rem(me + senders - ahead, senders)
        return send(
            payload_ref.at[source],
            received_ref.at[source],
            payload_send.at[ahead],
            payload_recv.at[ahead],
            place_of(source),
        )

    for ahead in range(1, senders):
        payload_copy(ahead).start()
    received_ref[me] = payload_ref[me]
    for ahead in range(1, senders):
        payload_arrival(ahead).wait_recv()

    padded = table_ref.shape[1]
    for part in range(7):
        data = received_ref[:, part, :]
        high = data.astype(BF16).astype(F32)
        rest = data - high
        middle = rest.astype(BF16).astype(F32)
        parts = [high, middle, rest - middle]
        if padded > 3 * senders:
            parts.append(jnp.zeros((padded - 3 * senders, LANES), F32))
        table_ref[part * LANES : (part + 1) * LANES, :] = (
            jnp.concatenate(parts, axis=0).T.astype(BF16)
        )

    def slots_of(index):
        k = index // pieces
        at = pl.multiple_of(lax.rem(index, pieces) * width, LANES)
        slots = slot_ref[k, :, pl.ds(at, width)]
        live = live_ref[k, :, pl.ds(at, width)]
        source = slots // LANES
        place = slots - source * LANES
        sender = lax.broadcasted_iota(jnp.int32, (senders, width), 0)
        chosen = jnp.where(sender == source, 1.0, 0.0).astype(F32)
        here = lax.broadcasted_iota(jnp.int32, (LANES, width), 0) == place
        return k, at, live, chosen, here

    def pick_step(index, carry):
        k, at, live, chosen, here = slots_of(index)
        picks = [chosen] * 3
        if padded > 3 * senders:
            picks.append(jnp.zeros((padded - 3 * senders, width), F32))
        picked = dot(table_ref[...], jnp.concatenate(picks, axis=0).astype(BF16), NN)
        rows = []
        for part in range(7):
            block = picked[part * LANES : (part + 1) * LANES]
            rows.append(jnp.sum(jnp.where(here, block, 0.0), axis=0, keepdims=True))
        rows[0] = rows[0] * live
        rows[1] = rows[1] * live
        rows.append(live)
        entry_ref[fft_at, k, :, pl.ds(at, width)] = jnp.concatenate(rows, axis=0)
        return carry

    lax.fori_loop(0, rounds, pick_step, 0, unroll=2)

    def entry_copy(ahead):
        return send(
            entry_ref.at[fft_at],
            entry_ref.at[fft_at],
            entry_send.at[ahead],
            entry_recv.at[ahead],
            (lax.rem(fft_at + ahead, owners), chan_at),
        )

    def entry_arrival(ahead):
        owner = lax.rem(fft_at + owners - ahead, owners)
        return send(
            entry_ref.at[owner],
            entry_ref.at[owner],
            entry_send.at[ahead],
            entry_recv.at[ahead],
            (owner, chan_at),
        )

    for ahead in range(1, owners):
        entry_copy(ahead).start()

    def locate(owner, index):
        piece = lax.rem(index, pieces)
        k = index // pieces
        channel = k // tiles_each
        column = (owner * tiles_each + lax.rem(k, tiles_each)) * tile_cols
        span = column // SPAN
        inner = column - span * SPAN
        at = pl.multiple_of(piece * width, LANES)
        return k, at, channel, span, inner

    def column_table(entries, inner):
        column = entries[5:6] + inner.astype(F32)
        half_width = entries[6:7] + 1.0
        rate = -1.0 / (0.72 * half_width * half_width)
        home = jnp.floor((column - 4.0) * (1.0 / LANES))
        local = column - home * LANES
        place = lax.broadcasted_iota(jnp.int32, (REACH, width), 0).astype(F32)
        distance = place - local
        offset = distance - entries[3:4]
        shape_value = jnp.exp(offset * offset * rate)
        table = jnp.where(jnp.abs(distance) <= half_width, shape_value, 0.0)
        high, low = split(table)
        rest = jnp.zeros((2 * LANES - REACH, width), BF16)
        which = lax.broadcasted_iota(jnp.int32, (GROUPS, width), 0).astype(F32)
        return high, low, rest, jnp.where(which == home, 1.0, 0.0)

    if gathered:
        grid_ref[...] = jnp.zeros_like(grid_ref)

    def grid_step(owner, index):
        k, at, channel, span, inner = locate(owner, index)
        entries = entry_ref[owner, k, :, pl.ds(at, width)]
        half_width = entries[6:7] + 1.0
        rate = -1.0 / (0.72 * half_width * half_width)
        band_row = lax.broadcasted_iota(jnp.int32, (BU, width), 0).astype(F32)
        distance = band_row - entries[4:5]
        offset = distance - entries[2:3]
        row_kernel = jnp.where(
            jnp.abs(distance) <= half_width, jnp.exp(offset * offset * rate), 0.0
        )
        phased = dot(band_ref[...], side3(row_kernel, 0), NN)
        row_ref[owner * rounds + index] = phased
        phased_re, phased_im = phased[:row_local], phased[row_local:]
        weight_re = entries[0:1] * phased_re - entries[1:2] * phased_im
        weight_im = entries[0:1] * phased_im + entries[1:2] * phased_re
        high, low, rest, home = column_table(entries, inner)
        table = jnp.concatenate(
            [
                jnp.concatenate([high, low, high], axis=1),
                jnp.concatenate([rest, rest, rest], axis=1),
            ],
            axis=0,
        )
        spread = jnp.concatenate(
            [
                jnp.broadcast_to(weight[i : i + 1], (GROUPS, width)) * home
                for weight in (weight_re, weight_im)
                for i in range(row_local)
            ],
            axis=0,
        )
        spread_high, spread_low = split(spread)
        spread = jnp.concatenate([spread_high, spread_high, spread_low], axis=1)
        wide = dot(spread, table, NT)
        block = wide[:, :LANES] + pltpu.roll(wide[:, LANES:], 1, 0)
        block = block.reshape(2, row_local, GROUPS, LANES)
        first_row = pl.multiple_of(channel * row_local, row_local)
        for part in range(2):
            spot = (
                pl.ds(first_row, row_local),
                pl.ds(pl.multiple_of(part * lead + span * GROUPS, GROUPS), GROUPS),
            )
            if gathered:
                grid_ref[spot] += block[part]
            else:
                grid_ref[spot] = block[part]

    def grid_owner(ahead, carry):
        owner = lax.rem(fft_at + owners - ahead, owners)

        @pl.when(ahead > 0)
        def _():
            entry_arrival(ahead).wait_recv()

        def step(index, inner_carry):
            grid_step(owner, index)
            return inner_carry

        lax.fori_loop(0, rounds, step, 0, unroll=2)
        return carry

    lax.fori_loop(0, owners, grid_owner, 0)
    for load in loads:
        load.wait()

    together = math.gcd(rows_total, 4)

    def image_step(index, carry):
        first_row = index * together
        cos, sin = twist_ref[0], twist_ref[1]
        cos_t, sin_t = twist_t_ref[0], twist_t_ref[1]
        columns = jnp.concatenate(
            [grid_ref[first_row + lane] for lane in range(together)], axis=1
        )
        stage = dot(first_ref[...], side3(columns, 0), NN)
        turned_back = []
        for lane in range(together):
            row = first_row + lane
            real = stage[:lead, lane * LANES : (lane + 1) * LANES]
            imag = stage[lead:, lane * LANES : (lane + 1) * LANES]
            turned = jnp.concatenate([real * cos + imag * sin, imag * cos - real * sin], axis=1)
            dirty = dot(second_ref[...], side3(turned, 1), NT) * dirty_scale
            level = threshold_ref[row // row_local]
            change = LOOP_GAIN * (dirty - jnp.clip(dirty, -level, level))
            halves = []
            for half in range(lead // LANES):
                spot = (
                    row // group,
                    pl.ds(half * group + lax.rem(row, group), LANES, stride=(lead // LANES) * group),
                )
                updated = model_ref[spot] + change[:, half * LANES : (half + 1) * LANES]
                updated_ref[spot] = updated
                halves.append(updated)
            image = jnp.concatenate(halves, axis=1)
            back = dot(third_ref[...], side3(image, 0), NN)
            real, imag = back[:LANES], back[LANES:]
            turned_back.append(
                jnp.concatenate(
                    [real * cos_t - imag * sin_t, real * sin_t + imag * cos_t], axis=1
                )
            )
        columns = dot(last_ref[...], side3(jnp.concatenate(turned_back, axis=0), 1), NT)
        for lane in range(together):
            grid_ref[first_row + lane] = columns[:, lane * LANES : (lane + 1) * LANES]
        return carry

    lax.fori_loop(0, rows_total // together, image_step, 0)
    store = pltpu.make_async_copy(updated_ref, updated_any, load_sem.at[3])
    store.start()

    def degrid_step(owner, index):
        k, at, channel, span, inner = locate(owner, index)
        entries = entry_ref[owner, k, :, pl.ds(at, width)]
        high, low, rest, home = column_table(entries, inner)
        table = jnp.concatenate([high, rest, low, rest, high, rest], axis=0)
        first_row = pl.multiple_of(channel * row_local, row_local)
        blocks = []
        for part in range(2):
            block = grid_ref[
                pl.ds(first_row, row_local),
                pl.ds(pl.multiple_of(part * lead + span * GROUPS, GROUPS), GROUPS),
            ]
            blocks.append(block.reshape(row_local * GROUPS, LANES))
        block = jnp.concatenate(blocks, axis=0)
        wide = jnp.concatenate([block, pltpu.roll(block, block.shape[0] - 1, 0)], axis=1)
        wide_high, wide_low = split(wide)
        sampled = dot(jnp.concatenate([wide_high, wide_high, wide_low], axis=1), table, NN)
        phased = row_ref[owner * rounds + index]
        total_re = jnp.zeros((GROUPS, width), F32)
        total_im = jnp.zeros((GROUPS, width), F32)
        for i in range(row_local):
            real = sampled[i * GROUPS : (i + 1) * GROUPS]
            imag = sampled[(row_local + i) * GROUPS : (row_local + i + 1) * GROUPS]
            turn_re = phased[i : i + 1]
            turn_im = phased[row_local + i : row_local + i + 1]
            total_re += turn_re * real + turn_im * imag
            total_im += turn_re * imag - turn_im * real
        predicted_ref[owner, k, :, pl.ds(at, width)] = jnp.concatenate(
            [
                jnp.sum(total_re * home, axis=0, keepdims=True) * back_scale,
                jnp.sum(total_im * home, axis=0, keepdims=True) * back_scale,
            ],
            axis=0,
        )

    def partial_copy(ahead):
        owner = lax.rem(fft_at + ahead, owners)
        return send(
            predicted_ref.at[owner],
            arrived_ref.at[ahead],
            partial_send.at[ahead],
            partial_recv.at[ahead],
            (owner, chan_at),
        )

    def degrid_owner(turn, carry):
        ahead = owners - 1 - turn
        owner = lax.rem(fft_at + ahead, owners)

        def step(index, inner_carry):
            degrid_step(owner, index)
            return inner_carry

        lax.fori_loop(0, rounds, step, 0, unroll=2)

        @pl.when(ahead > 0)
        def _():
            partial_copy(ahead).start()

        return carry

    lax.fori_loop(0, owners, degrid_owner, 0)
    for ahead in range(1, owners):
        partial_copy(ahead).wait_recv()

    def place_step(index, carry):
        k, at, live, chosen, here = slots_of(index)
        values = predicted_ref[fft_at, k, :, pl.ds(at, width)]
        for ahead in range(1, owners):
            values = values + arrived_ref[ahead, k, :, pl.ds(at, width)]
        values = values * live
        spread = jnp.concatenate(
            [jnp.where(here, values[part : part + 1], 0.0) for part in range(2)], axis=0
        )
        high, low = split(spread)
        chosen = chosen.astype(BF16)
        return carry + (dot(chosen, high, NT) + dot(chosen, low, NT))

    placed = lax.fori_loop(
        0, rounds, place_step, jnp.zeros((senders, 2 * LANES), F32), unroll=2
    )
    for part in range(2):
        outgoing_ref[:, part, :] = placed[:, part * LANES : (part + 1) * LANES]

    def return_copy(ahead):
        target = lax.rem(me + ahead, senders)
        return send(
            outgoing_ref.at[target],
            returned_ref.at[me],
            return_send.at[ahead],
            return_recv.at[ahead],
            place_of(target),
        )

    def return_arrival(ahead):
        source = lax.rem(me + senders - ahead, senders)
        return send(
            outgoing_ref.at[source],
            returned_ref.at[source],
            return_send.at[ahead],
            return_recv.at[ahead],
            place_of(source),
        )

    for ahead in range(1, senders):
        return_copy(ahead).start()
    returned_ref[me] = outgoing_ref[me]
    for ahead in range(1, senders):
        return_arrival(ahead).wait_recv()
    in_use = lax.broadcasted_iota(jnp.int32, (senders, LANES), 1) < count_ref[...]
    for part in range(2):
        difference = payload_ref[:, part, :] - returned_ref[:, part, :]
        residual_ref[part] = jnp.where(in_use, difference, 0.0)
    for ahead in range(1, senders):
        payload_copy(ahead).wait_send()
        return_copy(ahead).wait_send()
    for ahead in range(1, owners):
        entry_copy(ahead).wait_send()
        partial_copy(ahead).wait_send()
    store.wait()


def imaging_cycle(payload, slots, live, counts, band, model, threshold, plan, grid_side, owners):
    senders = payload.shape[0]
    lists, _, cap = slots.shape
    _, row_local, _, _, width, group = plan[:6]
    lead = grid_side // LANES
    rows_total = model.shape[0] * group
    steps = owners * lists * (cap // width)
    padded = -(-3 * senders // LANES) * LANES
    first, second, third, last, twist, twist_t = (
        jnp.asarray(table) for table in transform_tables(grid_side)
    )
    in_vmem = pl.BlockSpec(memory_space=pltpu.VMEM)
    anywhere = pl.BlockSpec(memory_space=pl.ANY)
    return pl.pallas_call(
        functools.partial(cycle_kernel, plan),
        out_shape=(
            jax.ShapeDtypeStruct(model.shape, F32),
            jax.ShapeDtypeStruct((2, senders, LANES), F32),
        ),
        in_specs=[in_vmem] * 5
        + [pl.BlockSpec(memory_space=pltpu.SMEM)]
        + [in_vmem] * 4
        + [anywhere] * 3,
        out_specs=(anywhere, in_vmem),
        scratch_shapes=[
            pltpu.VMEM(payload.shape, F32),
            pltpu.VMEM((7 * LANES, padded), BF16),
            pltpu.VMEM((owners, lists, 8, cap), F32),
            pltpu.VMEM(first.shape, BF16),
            pltpu.VMEM(last.shape, BF16),
            pltpu.VMEM(model.shape, F32),
            pltpu.VMEM(model.shape, F32),
            pltpu.VMEM((rows_total, 2 * lead, LANES), F32),
            pltpu.VMEM((steps, 2 * row_local, width), F32),
            pltpu.VMEM((owners, lists, 2, cap), F32),
            pltpu.VMEM((owners, lists, 2, cap), F32),
            pltpu.VMEM((senders, 2, LANES), F32),
            pltpu.VMEM((senders, 2, LANES), F32),
            pltpu.SemaphoreType.DMA((4,)),
            pltpu.SemaphoreType.DMA((senders,)),
            pltpu.SemaphoreType.DMA((senders,)),
            pltpu.SemaphoreType.DMA((owners,)),
            pltpu.SemaphoreType.DMA((owners,)),
            pltpu.SemaphoreType.DMA((owners,)),
            pltpu.SemaphoreType.DMA((owners,)),
            pltpu.SemaphoreType.DMA((senders,)),
            pltpu.SemaphoreType.DMA((senders,)),
        ],
        compiler_params=pltpu.CompilerParams(
            vmem_limit_bytes=VMEM_BYTES, collective_id=0, has_side_effects=True
        ),
        name="imaging_cycle",
    )(
        payload, slots, live, counts, band, threshold,
        second, third, twist, twist_t, first, last, model,
    )


def per_device(
    visibilities,
    positions,
    cell_row,
    cell_column,
    kernel_class,
    send_counts,
    tile_lists,
    tile_counts,
    model_image,
    threshold,
):
    fft_devices = lax.axis_size("fft")
    chan_devices = lax.axis_size("chan")
    senders = fft_devices * chan_devices
    local_tiles = tile_lists.shape[1]
    tile_cap = tile_lists.shape[2]
    chan_local, row_local, grid_side = model_image.shape
    tiles_each = local_tiles // chan_local
    facet_rows = row_local * fft_devices
    tile_cols = grid_side // (fft_devices * tiles_each)
    dirty_scale = 1.0 / math.sqrt(fft_devices * tiles_each * tile_cap)
    back_scale = 0.5 / math.sqrt(facet_rows * grid_side)
    width = 384 if tile_cap % 384 == 0 else LANES
    group = math.gcd(row_local, 8)

    labels = jnp.stack([cell_row, cell_column, kernel_class], axis=1).astype(F32)
    blank = jnp.zeros_like(visibilities[:, :1])
    payload = jnp.concatenate([visibilities, positions, labels, blank], axis=1)[0]
    payload = payload.transpose(1, 0, 2)
    slots = tile_lists[0][:, None, :]
    live = jnp.arange(tile_cap, dtype=jnp.int32)[None, :] < tile_counts[0][:, None]
    live = live.astype(F32)[:, None, :]

    band_index = np.arange(facet_rows)[:, None] * (grid_side // 2 + np.arange(BU))[None, :]
    band_cos, band_sin = unit(band_index, facet_rows)
    band = np.stack([band_cos, -band_sin]).reshape(2, fft_devices, row_local, BU)
    band = table3(band.transpose(1, 0, 2, 3).reshape(fft_devices, 2 * row_local, BU))
    band = lax.dynamic_index_in_dim(
        jnp.asarray(band), lax.axis_index("fft"), axis=0, keepdims=False
    )
    lanes_total = grid_side // LANES
    rows_total = chan_local * row_local
    model = model_image.reshape(rows_total // group, group, lanes_total, LANES)
    model = model.transpose(0, 2, 1, 3).reshape(rows_total // group, lanes_total * group, LANES)
    plan = (
        chan_devices, row_local, tiles_each, tile_cols, width, group, dirty_scale, back_scale
    )
    updated, residuals = imaging_cycle(
        payload,
        slots,
        live,
        send_counts.reshape(senders, 1),
        band,
        model,
        threshold,
        plan,
        grid_side,
        fft_devices,
    )
    updated = updated.reshape(rows_total // group, lanes_total, group, LANES)
    updated = updated.transpose(0, 2, 1, 3).reshape(model_image.shape)
    return (updated, residuals[None])


def solution(mesh):
    placed = (
        P(("fft", "chan"), None, None, None),
        P(("fft", "chan"), None, None, None),
        P(("fft", "chan"), None, None),
        P(("fft", "chan"), None, None),
        P(("fft", "chan"), None, None),
        P(("fft", "chan"), None),
        P(("fft", "chan"), None, None),
        P(("fft", "chan"), None),
        P("chan", "fft", None),
        P("chan"),
    )
    return jax.shard_map(
        per_device,
        mesh=mesh,
        in_specs=placed,
        out_specs=(P("chan", "fft", None), P(("fft", "chan"), None, None, None)),
        check_vma=False,
    )
```

```python
import functools
import math

import jax
import jax.numpy as jnp
import ml_dtypes
import numpy as np
from jax import lax
from jax.experimental import pallas as pl
from jax.experimental.pallas import tpu as pltpu
from jax.sharding import PartitionSpec as P

BU = 64
LOOP_GAIN = 0.7
LANES = 128
GROUPS = 8
SPAN = GROUPS * LANES
REACH = 144
VMEM_BYTES = 56 * 1024 * 1024
F32 = jnp.float32
BF16 = jnp.bfloat16
NN = (((1,), (0,)), ((), ()))
NT = (((1,), (1,)), ((), ()))


def split_table(table):
    table = np.asarray(table, np.float32)
    high = table.astype(ml_dtypes.bfloat16)
    low = (table - high.astype(np.float32)).astype(ml_dtypes.bfloat16)
    return high, low


def table3(table):
    high, low = split_table(table)
    return np.concatenate([high, high, low], axis=-1)


def split(value):
    high = value.astype(BF16)
    low = (value - high.astype(F32)).astype(BF16)
    return high, low


def dot(a, b, dims):
    return lax.dot_general(a, b, dims, preferred_element_type=F32)


def side3(value, axis):
    high, low = split(value)
    return jnp.concatenate([high, low, high], axis=axis)


def unit(product, modulus):
    angle = 2.0 * np.pi / modulus * (product % modulus)
    return np.cos(angle), np.sin(angle)


def transform_tables(grid_side):
    lead = grid_side // LANES
    long_index, short_index = np.arange(lead), np.arange(LANES)
    cos1, sin1 = unit(long_index[:, None] * long_index[None, :], lead)
    cos2, sin2 = unit(short_index[:, None] * short_index[None, :], LANES)
    twist_cos, twist_sin = unit(long_index[:, None] * short_index[None, :], grid_side)
    first = np.block([[cos1, sin1], [-sin1, cos1]])
    second = np.concatenate([cos2, sin2], axis=1)
    third = np.concatenate([cos2, sin2], axis=0)
    last = np.block([[cos1, -sin1], [sin1, cos1]])
    return (
        table3(first),
        table3(second),
        table3(third),
        table3(last),
        np.stack([twist_cos, twist_sin]).astype(np.float32),
        np.stack([twist_cos.T, twist_sin.T]).astype(np.float32),
    )


def cycle_kernel(
    plan,
    payload_ref,
    slot_ref,
    live_ref,
    count_ref,
    band_ref,
    threshold_ref,
    second_ref,
    third_ref,
    twist_ref,
    twist_t_ref,
    first_any,
    last_any,
    model_any,
    updated_any,
    residual_ref,
    received_ref,
    table_ref,
    entry_ref,
    first_ref,
    last_ref,
    model_ref,
    updated_ref,
    grid_ref,
    row_ref,
    predicted_ref,
    arrived_ref,
    outgoing_ref,
    returned_ref,
    load_sem,
    payload_send,
    payload_recv,
    entry_send,
    entry_recv,
    partial_send,
    partial_recv,
    return_send,
    return_recv,
):
    (chan_devices, row_local, tiles_each, tile_cols, width, group, dirty_scale, back_scale) = plan
    owners, lists, _, cap = entry_ref.shape
    senders = owners * chan_devices
    rows_total, lead2, _ = grid_ref.shape
    lead = lead2 // 2
    pieces = cap // width
    rounds = lists * pieces
    gathered = tile_cols < SPAN or pieces > 1
    fft_at, chan_at = lax.axis_index("fft"), lax.axis_index("chan")
    me = fft_at * chan_devices + chan_at

    def place_of(device):
        return (device // chan_devices, lax.rem(device, chan_devices))

    def send(source, target, send_sem, recv_sem, device):
        return pltpu.make_async_remote_copy(
            src_ref=source,
            dst_ref=target,
            send_sem=send_sem,
            recv_sem=recv_sem,
            device_id=device,
            device_id_type=pl.DeviceIdType.MESH,
        )

    loads = [
        pltpu.make_async_copy(source, target, load_sem.at[i])
        for i, (source, target) in enumerate(
            ((model_any, model_ref), (first_any, first_ref), (last_any, last_ref))
        )
    ]
    for load in loads:
        load.start()

    barrier = pltpu.get_barrier_semaphore()
    for ahead in range(1, senders):
        pl.semaphore_signal(
            barrier,
            inc=1,
            device_id=place_of(lax.rem(me + ahead, senders)),
            device_id_type=pl.DeviceIdType.MESH,
        )
    pl.semaphore_wait(barrier, senders - 1)

    def payload_copy(ahead):
        target = lax.rem(me + ahead, senders)
        return send(
            payload_ref.at[target],
            received_ref.at[me],
            payload_send.at[ahead],
            payload_recv.at[ahead],
            place_of(target),
        )

    def payload_arrival(ahead):
        source = lax.rem(me + senders - ahead, senders)
        return send(
            payload_ref.at[source],
            received_ref.at[source],
            payload_send.at[ahead],
            payload_recv.at[ahead],
            place_of(source),
        )

    for ahead in range(1, senders):
        payload_copy(ahead).start()
    received_ref[me] = payload_ref[me]
    for ahead in range(1, senders):
        payload_arrival(ahead).wait_recv()

    padded = table_ref.shape[1]
    for part in range(7):
        data = received_ref[:, part, :]
        high = data.astype(BF16).astype(F32)
        rest = data - high
        middle = rest.astype(BF16).astype(F32)
        parts = [high, middle, rest - middle]
        if padded > 3 * senders:
            parts.append(jnp.zeros((padded - 3 * senders, LANES), F32))
        table_ref[part * LANES : (part + 1) * LANES, :] = (
            jnp.concatenate(parts, axis=0).T.astype(BF16)
        )

    def slots_of(index):
        k = index // pieces
        at = pl.multiple_of(lax.rem(index, pieces) * width, LANES)
        slots = slot_ref[pl.ds(k, 1), pl.ds(at, width)]
        entry = lax.broadcasted_iota(jnp.int32, (1, width), 1) + at
        live = jnp.where(entry < live_ref[k], 1.0, 0.0)
        source = slots // LANES
        place = slots - source * LANES
        sender = lax.broadcasted_iota(jnp.int32, (senders, width), 0)
        chosen = jnp.where(sender == source, 1.0, 0.0).astype(F32)
        here = lax.broadcasted_iota(jnp.int32, (LANES, width), 0) == place
        return k, at, live, chosen, here

    def pick_step(index, carry):
        k, at, live, chosen, here = slots_of(index)
        picks = [chosen] * 3
        if padded > 3 * senders:
            picks.append(jnp.zeros((padded - 3 * senders, width), F32))
        picked = dot(table_ref[...], jnp.concatenate(picks, axis=0).astype(BF16), NN)
        rows = []
        for part in range(7):
            block = picked[part * LANES : (part + 1) * LANES]
            rows.append(jnp.sum(jnp.where(here, block, 0.0), axis=0, keepdims=True))
        rows[0] = rows[0] * live
        rows[1] = rows[1] * live
        rows.append(live)
        entry_ref[fft_at, k, :, pl.ds(at, width)] = jnp.concatenate(rows, axis=0)
        return carry

    lax.fori_loop(0, rounds, pick_step, 0, unroll=2)

    def entry_copy(ahead):
        return send(
            entry_ref.at[fft_at],
            entry_ref.at[fft_at],
            entry_send.at[ahead],
            entry_recv.at[ahead],
            (lax.rem(fft_at + ahead, owners), chan_at),
        )

    def entry_arrival(ahead):
        owner = lax.rem(fft_at + owners - ahead, owners)
        return send(
            entry_ref.at[owner],
            entry_ref.at[owner],
            entry_send.at[ahead],
            entry_recv.at[ahead],
            (owner, chan_at),
        )

    for ahead in range(1, owners):
        entry_copy(ahead).start()

    def locate(owner, index):
        piece = lax.rem(index, pieces)
        k = index // pieces
        channel = k // tiles_each
        column = (owner * tiles_each + lax.rem(k, tiles_each)) * tile_cols
        span = column // SPAN
        inner = column - span * SPAN
        at = pl.multiple_of(piece * width, LANES)
        return k, at, channel, span, inner

    def column_table(entries, inner):
        column = entries[5:6] + inner.astype(F32)
        half_width = entries[6:7] + 1.0
        rate = -1.0 / (0.72 * half_width * half_width)
        home = jnp.floor((column - 4.0) * (1.0 / LANES))
        local = column - home * LANES
        place = lax.broadcasted_iota(jnp.int32, (REACH, width), 0).astype(F32)
        distance = place - local
        offset = distance - entries[3:4]
        shape_value = jnp.exp(offset * offset * rate)
        table = jnp.where(jnp.abs(distance) <= half_width, shape_value, 0.0)
        high, low = split(table)
        rest = jnp.zeros((2 * LANES - REACH, width), BF16)
        which = lax.broadcasted_iota(jnp.int32, (GROUPS, width), 0).astype(F32)
        return high, low, rest, jnp.where(which == home, 1.0, 0.0)

    if gathered:
        grid_ref[...] = jnp.zeros_like(grid_ref)

    def grid_step(owner, index):
        k, at, channel, span, inner = locate(owner, index)
        entries = entry_ref[owner, k, :, pl.ds(at, width)]
        half_width = entries[6:7] + 1.0
        rate = -1.0 / (0.72 * half_width * half_width)
        band_row = lax.broadcasted_iota(jnp.int32, (BU, width), 0).astype(F32)
        distance = band_row - entries[4:5]
        offset = distance - entries[2:3]
        row_kernel = jnp.where(
            jnp.abs(distance) <= half_width, jnp.exp(offset * offset * rate), 0.0
        )
        phased = dot(band_ref[fft_at], side3(row_kernel, 0), NN)
        row_ref[owner * rounds + index] = phased
        phased_re, phased_im = phased[:row_local], phased[row_local:]
        weight_re = entries[0:1] * phased_re - entries[1:2] * phased_im
        weight_im = entries[0:1] * phased_im + entries[1:2] * phased_re
        high, low, rest, home = column_table(entries, inner)
        table = jnp.concatenate(
            [
                jnp.concatenate([high, low, high], axis=1),
                jnp.concatenate([rest, rest, rest], axis=1),
            ],
            axis=0,
        )
        spread = jnp.concatenate(
            [
                jnp.broadcast_to(weight[i : i + 1], (GROUPS, width)) * home
                for weight in (weight_re, weight_im)
                for i in range(row_local)
            ],
            axis=0,
        )
        spread_high, spread_low = split(spread)
        spread = jnp.concatenate([spread_high, spread_high, spread_low], axis=1)
        wide = dot(spread, table, NT)
        block = wide[:, :LANES] + pltpu.roll(wide[:, LANES:], 1, 0)
        block = block.reshape(2, row_local, GROUPS, LANES)
        first_row = pl.multiple_of(channel * row_local, row_local)
        for part in range(2):
            spot = (
                pl.ds(first_row, row_local),
                pl.ds(pl.multiple_of(part * lead + span * GROUPS, GROUPS), GROUPS),
            )
            if gathered:
                grid_ref[spot] += block[part]
            else:
                grid_ref[spot] = block[part]

    def grid_owner(ahead, carry):
        owner = lax.rem(fft_at + owners - ahead, owners)

        @pl.when(ahead > 0)
        def _():
            entry_arrival(ahead).wait_recv()

        def step(index, inner_carry):
            grid_step(owner, index)
            return inner_carry

        lax.fori_loop(0, rounds, step, 0, unroll=4)
        return carry

    lax.fori_loop(0, owners, grid_owner, 0)
    for load in loads:
        load.wait()

    together = math.gcd(rows_total, 4)

    def image_step(index, carry):
        first_row = index * together
        cos, sin = twist_ref[0], twist_ref[1]
        cos_t, sin_t = twist_t_ref[0], twist_t_ref[1]
        columns = jnp.concatenate(
            [grid_ref[first_row + lane] for lane in range(together)], axis=1
        )
        stage = dot(first_ref[...], side3(columns, 0), NN)
        turned_back = []
        for lane in range(together):
            row = first_row + lane
            real = stage[:lead, lane * LANES : (lane + 1) * LANES]
            imag = stage[lead:, lane * LANES : (lane + 1) * LANES]
            turned = jnp.concatenate([real * cos + imag * sin, imag * cos - real * sin], axis=1)
            dirty = dot(second_ref[...], side3(turned, 1), NT) * dirty_scale
            level = threshold_ref[row // row_local]
            change = LOOP_GAIN * (dirty - jnp.clip(dirty, -level, level))
            halves = []
            for half in range(lead // LANES):
                spot = (
                    row // group,
                    pl.ds(half * group + lax.rem(row, group), LANES, stride=(lead // LANES) * group),
                )
                updated = model_ref[spot] + change[:, half * LANES : (half + 1) * LANES]
                updated_ref[spot] = updated
                halves.append(updated)
            image = jnp.concatenate(halves, axis=1)
            back = dot(third_ref[...], side3(image, 0), NN)
            real, imag = back[:LANES], back[LANES:]
            turned_back.append(
                jnp.concatenate(
                    [real * cos_t - imag * sin_t, real * sin_t + imag * cos_t], axis=1
                )
            )
        columns = dot(last_ref[...], side3(jnp.concatenate(turned_back, axis=0), 1), NT)
        for lane in range(together):
            grid_ref[first_row + lane] = columns[:, lane * LANES : (lane + 1) * LANES]
        return carry

    lax.fori_loop(0, rows_total // together, image_step, 0)
    store = pltpu.make_async_copy(updated_ref, updated_any, load_sem.at[3])
    store.start()

    def degrid_step(owner, index):
        k, at, channel, span, inner = locate(owner, index)
        entries = entry_ref[owner, k, :, pl.ds(at, width)]
        high, low, rest, home = column_table(entries, inner)
        table = jnp.concatenate([high, rest, low, rest, high, rest], axis=0)
        first_row = pl.multiple_of(channel * row_local, row_local)
        blocks = []
        for part in range(2):
            block = grid_ref[
                pl.ds(first_row, row_local),
                pl.ds(pl.multiple_of(part * lead + span * GROUPS, GROUPS), GROUPS),
            ]
            blocks.append(block.reshape(row_local * GROUPS, LANES))
        block = jnp.concatenate(blocks, axis=0)
        wide = jnp.concatenate([block, pltpu.roll(block, block.shape[0] - 1, 0)], axis=1)
        wide_high, wide_low = split(wide)
        sampled = dot(jnp.concatenate([wide_high, wide_high, wide_low], axis=1), table, NN)
        phased = row_ref[owner * rounds + index]
        total_re = jnp.zeros((GROUPS, width), F32)
        total_im = jnp.zeros((GROUPS, width), F32)
        for i in range(row_local):
            real = sampled[i * GROUPS : (i + 1) * GROUPS]
            imag = sampled[(row_local + i) * GROUPS : (row_local + i + 1) * GROUPS]
            turn_re = phased[i : i + 1]
            turn_im = phased[row_local + i : row_local + i + 1]
            total_re += turn_re * real + turn_im * imag
            total_im += turn_re * imag - turn_im * real
        predicted_ref[owner, k, :, pl.ds(at, width)] = jnp.concatenate(
            [
                jnp.sum(total_re * home, axis=0, keepdims=True) * back_scale,
                jnp.sum(total_im * home, axis=0, keepdims=True) * back_scale,
            ],
            axis=0,
        )

    def partial_copy(ahead):
        owner = lax.rem(fft_at + ahead, owners)
        return send(
            predicted_ref.at[owner],
            arrived_ref.at[ahead],
            partial_send.at[ahead],
            partial_recv.at[ahead],
            (owner, chan_at),
        )

    def degrid_owner(turn, carry):
        ahead = owners - 1 - turn
        owner = lax.rem(fft_at + ahead, owners)

        def step(index, inner_carry):
            degrid_step(owner, index)
            return inner_carry

        lax.fori_loop(0, rounds, step, 0, unroll=4)

        @pl.when(ahead > 0)
        def _():
            partial_copy(ahead).start()

        return carry

    lax.fori_loop(0, owners, degrid_owner, 0)
    for ahead in range(1, owners):
        partial_copy(ahead).wait_recv()

    def place_step(index, carry):
        k, at, live, chosen, here = slots_of(index)
        values = predicted_ref[fft_at, k, :, pl.ds(at, width)]
        for ahead in range(1, owners):
            values = values + arrived_ref[ahead, k, :, pl.ds(at, width)]
        values = values * live
        spread = jnp.concatenate(
            [jnp.where(here, values[part : part + 1], 0.0) for part in range(2)], axis=0
        )
        high, low = split(spread)
        chosen = chosen.astype(BF16)
        return carry + (dot(chosen, high, NT) + dot(chosen, low, NT))

    placed = lax.fori_loop(
        0, rounds, place_step, jnp.zeros((senders, 2 * LANES), F32), unroll=2
    )
    for part in range(2):
        outgoing_ref[:, part, :] = placed[:, part * LANES : (part + 1) * LANES]

    def return_copy(ahead):
        target = lax.rem(me + ahead, senders)
        return send(
            outgoing_ref.at[target],
            returned_ref.at[me],
            return_send.at[ahead],
            return_recv.at[ahead],
            place_of(target),
        )

    def return_arrival(ahead):
        source = lax.rem(me + senders - ahead, senders)
        return send(
            outgoing_ref.at[source],
            returned_ref.at[source],
            return_send.at[ahead],
            return_recv.at[ahead],
            place_of(source),
        )

    for ahead in range(1, senders):
        return_copy(ahead).start()
    returned_ref[me] = outgoing_ref[me]
    for ahead in range(1, senders):
        return_arrival(ahead).wait_recv()
    in_use = lax.broadcasted_iota(jnp.int32, (senders, LANES), 1) < count_ref[...]
    for part in range(2):
        difference = payload_ref[:, part, :] - returned_ref[:, part, :]
        residual_ref[part] = jnp.where(in_use, difference, 0.0)
    for ahead in range(1, senders):
        payload_copy(ahead).wait_send()
        return_copy(ahead).wait_send()
    for ahead in range(1, owners):
        entry_copy(ahead).wait_send()
        partial_copy(ahead).wait_send()
    store.wait()


def imaging_cycle(payload, slots, live, counts, band, model, threshold, plan, grid_side, owners):
    senders = payload.shape[0]
    lists, cap = slots.shape
    _, row_local, _, _, width, group = plan[:6]
    lead = grid_side // LANES
    rows_total = model.shape[0] * group
    steps = owners * lists * (cap // width)
    padded = -(-3 * senders // LANES) * LANES
    first, second, third, last, twist, twist_t = (
        jnp.asarray(table) for table in transform_tables(grid_side)
    )
    in_vmem = pl.BlockSpec(memory_space=pltpu.VMEM)
    in_smem = pl.BlockSpec(memory_space=pltpu.SMEM)
    anywhere = pl.BlockSpec(memory_space=pl.ANY)
    return pl.pallas_call(
        functools.partial(cycle_kernel, plan),
        out_shape=(
            jax.ShapeDtypeStruct(model.shape, F32),
            jax.ShapeDtypeStruct((2, senders, LANES), F32),
        ),
        in_specs=[in_vmem, in_vmem, in_smem, in_vmem, in_vmem, in_smem]
        + [in_vmem] * 4
        + [anywhere] * 3,
        out_specs=(anywhere, in_vmem),
        scratch_shapes=[
            pltpu.VMEM(payload.shape, F32),
            pltpu.VMEM((7 * LANES, padded), BF16),
            pltpu.VMEM((owners, lists, 8, cap), F32),
            pltpu.VMEM(first.shape, BF16),
            pltpu.VMEM(last.shape, BF16),
            pltpu.VMEM(model.shape, F32),
            pltpu.VMEM(model.shape, F32),
            pltpu.VMEM((rows_total, 2 * lead, LANES), F32),
            pltpu.VMEM((steps, 2 * row_local, width), F32),
            pltpu.VMEM((owners, lists, 2, cap), F32),
            pltpu.VMEM((owners, lists, 2, cap), F32),
            pltpu.VMEM((senders, 2, LANES), F32),
            pltpu.VMEM((senders, 2, LANES), F32),
            pltpu.SemaphoreType.DMA((4,)),
            pltpu.SemaphoreType.DMA((senders,)),
            pltpu.SemaphoreType.DMA((senders,)),
            pltpu.SemaphoreType.DMA((owners,)),
            pltpu.SemaphoreType.DMA((owners,)),
            pltpu.SemaphoreType.DMA((owners,)),
            pltpu.SemaphoreType.DMA((owners,)),
            pltpu.SemaphoreType.DMA((senders,)),
            pltpu.SemaphoreType.DMA((senders,)),
        ],
        compiler_params=pltpu.CompilerParams(
            vmem_limit_bytes=VMEM_BYTES, collective_id=0, has_side_effects=True
        ),
        name="imaging_cycle",
    )(
        payload, slots, live, counts, band, threshold,
        second, third, twist, twist_t, first, last, model,
    )


def per_device(
    visibilities,
    positions,
    cell_row,
    cell_column,
    kernel_class,
    send_counts,
    tile_lists,
    tile_counts,
    model_image,
    threshold,
):
    fft_devices = lax.axis_size("fft")
    chan_devices = lax.axis_size("chan")
    senders = fft_devices * chan_devices
    local_tiles = tile_lists.shape[1]
    tile_cap = tile_lists.shape[2]
    chan_local, row_local, grid_side = model_image.shape
    tiles_each = local_tiles // chan_local
    facet_rows = row_local * fft_devices
    tile_cols = grid_side // (fft_devices * tiles_each)
    dirty_scale = 1.0 / math.sqrt(fft_devices * tiles_each * tile_cap)
    back_scale = 0.5 / math.sqrt(facet_rows * grid_side)
    width = 384 if tile_cap % 384 == 0 else LANES
    group = math.gcd(row_local, 8)

    labels = jnp.stack([cell_row, cell_column, kernel_class], axis=1).astype(F32)
    blank = jnp.zeros_like(visibilities[:, :1])
    payload = jnp.concatenate([visibilities, positions, labels, blank], axis=1)[0]
    payload = payload.transpose(1, 0, 2)
    band_index = np.arange(facet_rows)[:, None] * (grid_side // 2 + np.arange(BU))[None, :]
    band_cos, band_sin = unit(band_index, facet_rows)
    band = np.stack([band_cos, -band_sin]).reshape(2, fft_devices, row_local, BU)
    band = table3(band.transpose(1, 0, 2, 3).reshape(fft_devices, 2 * row_local, BU))
    lanes_total = grid_side // LANES
    rows_total = chan_local * row_local
    model = model_image.reshape(rows_total // group, group, lanes_total, LANES)
    model = model.transpose(0, 2, 1, 3).reshape(rows_total // group, lanes_total * group, LANES)
    plan = (
        chan_devices, row_local, tiles_each, tile_cols, width, group, dirty_scale, back_scale
    )
    updated, residuals = imaging_cycle(
        payload,
        tile_lists[0],
        tile_counts[0],
        send_counts.reshape(senders, 1),
        jnp.asarray(band),
        model,
        threshold,
        plan,
        grid_side,
        fft_devices,
    )
    updated = updated.reshape(rows_total // group, lanes_total, group, LANES)
    updated = updated.transpose(0, 2, 1, 3).reshape(model_image.shape)
    return (updated, residuals[None])


def solution(mesh):
    placed = (
        P(("fft", "chan"), None, None, None),
        P(("fft", "chan"), None, None, None),
        P(("fft", "chan"), None, None),
        P(("fft", "chan"), None, None),
        P(("fft", "chan"), None, None),
        P(("fft", "chan"), None),
        P(("fft", "chan"), None, None),
        P(("fft", "chan"), None),
        P("chan", "fft", None),
        P("chan"),
    )
    return jax.shard_map(
        per_device,
        mesh=mesh,
        in_specs=placed,
        out_specs=(P("chan", "fft", None), P(("fft", "chan"), None, None, None)),
        check_vma=False,
    )
```
